32 devices in a mesh: lat: 4 (over y, x), lon: 8 (over z, core).
Axes of the slice: x: 2, y: 2, z: 4, core: 2. Of those that a mesh axis runs over, the one named last changes fastest.
Arguments:
- features: bfloat16 [384, 256, 256], P('lat', 'lon'), may hold values from -6 to 6
- quad_weights: float32 [384, 3, 129], P('lat'), may hold values from -6 to 6
- cycle_index: int32 [384, 3, 129], P('lat'), may hold values from 0 to 8
- widths: int32 [384], P('lat'), may hold values from 1 to 64, as said below
- mix_weight: bfloat16 [9, 256, 256], replicated, may hold values from -0.125 to 0.125
Outputs:
- mixed: bfloat16 [384, 256, 256], P('lat', 'lon')
The draws below stay inside these ranges and needn't reach their ends.
Inputs may be any that keep to these rules, and one draw needn't show every extreme that they name: Rows within 8 rows of either end of the grid have widths above 32; rows 0 and 383 have exactly 64. All other rows have widths of at most 16, which row 8 reaches.
All inputs are finite; a program needn't handle non-finite values.
Results may differ from the reference program's by a relative error of at most 0.0031.
Values may be sent and summed in bfloat16 or wider, within the bound.
A program may use at most 128 MiB of HBM per device.

```python
import jax
import jax.numpy as jnp
from jax import lax

C = 256
NB = 9
POLAR = 8
LON_DEV = 32
WMAX = 64
NEAR = 16
NLAT = 384
NLON = 256
N_LON = 8


def draw_widths(key, part):
    first_key = jax.random.fold_in(key, 11)
    second_key = jax.random.fold_in(key, 23)
    rows = jnp.arange(NLAT).astype(jnp.int32)
    distance = jnp.minimum(rows, NLAT - 1 - rows)
    far_width = WMAX - jax.random.randint(first_key, (NLAT,), 0, LON_DEV)
    far_width = jnp.where(distance == 0, WMAX, far_width)
    near_width = jax.random.randint(second_key, (NLAT,), 1, NEAR + 1)
    near_width = jnp.where(rows == POLAR, NEAR, near_width)
    return jnp.where(distance < POLAR, far_width, near_width).astype(jnp.int32)


def with_ends(entries, stream_key, smallest, largest):
    extent = entries.shape
    spot = [jax.random.randint(jax.random.fold_in(stream_key, axis), (), 0, extent[axis]) for axis in range(len(extent))]
    entries = entries.at[tuple(spot)].set(smallest)
    longest = extent.index(max(extent))
    spot[longest] = (spot[longest] + 1) % extent[longest]
    return entries.at[tuple(spot)].set(largest)


def block_scale(key, dims, cuts, least, high):
    loudness = 1.0
    for position, parts in cuts:
        heights = jax.random.uniform(jax.random.fold_in(jax.random.fold_in(key, 6), position), (parts,), jnp.float32, least / len(cuts), high / len(cuts))
        loudness = loudness * jnp.repeat(jnp.exp(heights), dims[position] // parts).reshape((-1,) + (1,) * (len(dims) - 1 - position))
    return loudness


def centred(stream_key, dims, spread, limit, shards=(), held_as=jnp.bfloat16):
    values = spread * jax.random.normal(stream_key, dims, jnp.float32)
    if shards:
        values = values * block_scale(stream_key, dims, shards, -0.22, 0.18)
    return jnp.clip(values, -limit, limit).astype(held_as)


def setup_inputs(seed: int = 0) -> dict:
    arg_keys = jax.random.split(jax.random.key(seed), 6)
    features = centred(arg_keys[0], (NLAT, NLON, C), 1.0, 6.0, ((0, 4), (1, 8)))
    quad_weights = centred(arg_keys[1], (NLAT, 3, 2 * WMAX + 1), 1.0, 6.0, ((0, 4),), jnp.float32)
    cycle_index = with_ends(jax.random.randint(arg_keys[2], (NLAT, 3, 2 * WMAX + 1), 0, NB), jax.random.fold_in(arg_keys[2], 1), 0, NB - 1).astype(jnp.int32)
    widths = draw_widths(jax.random.fold_in(arg_keys[5], 71), 0)
    mix_weight = centred(arg_keys[4], (NB, C, C), (NB * C) ** -0.5, 0.125)
    return dict(features=features, quad_weights=quad_weights, cycle_index=cycle_index, widths=widths, mix_weight=mix_weight)


def basis_table(quad_weights, cycle_index, widths, count):
    offsets = jnp.arange(quad_weights.shape[2]).astype(jnp.int32) - quad_weights.shape[2] // 2
    inside = jnp.abs(offsets)[None, None, :] <= widths[:, None, None]
    member = cycle_index[:, None, :, :] == jnp.arange(count).astype(jnp.int32)[None, :, None, None]
    scale_row = 1.0 / jnp.sqrt(3.0 * (2.0 * widths.astype(jnp.float32) + 1.0))
    values = jnp.where(member & inside[:, None, :, :], quad_weights[:, None, :, :], jnp.float32(0.0))
    return (values * scale_row[:, None, None, None]).astype(jnp.bfloat16)

def toeplitz(values, columns):
    length = values.shape[-1]
    width_all = length - 1 + columns
    padded_values = jnp.concatenate([values, jnp.zeros(values.shape[:-1] + (columns,), values.dtype)], -1)
    tiled = jnp.tile(padded_values, (1,) * (values.ndim - 1) + (columns,))
    flat = tiled[..., :columns * width_all]
    return flat.reshape(values.shape[:-1] + (columns, width_all))

def reference(features, quad_weights, cycle_index, widths, mix_weight):
    count = mix_weight.shape[0]
    basis_values = basis_table(quad_weights, cycle_index, widths, count)
    padded = jnp.pad(features, ((1, 1), (0, 0), (0, 0)))
    weights_wide = mix_weight.astype(jnp.float32)

    def make_row(span):

        def row_out(row):
            rows_three = lax.dynamic_slice_in_dim(padded, row, 3, 0)
            values = lax.dynamic_index_in_dim(basis_values, row, 0, keepdims=False)
            values = values[:, :, WMAX - span:WMAX + span + 1]
            extended = jnp.concatenate([rows_three[:, NLON - span:], rows_three, rows_three[:, :span]], 1)
            starts = (jnp.arange(N_LON) * LON_DEV).astype(jnp.int32)
            index_grid = starts[:, None] + jnp.arange(LON_DEV + 2 * span).astype(jnp.int32)[None, :]
            windows = extended[:, index_grid]
            kernel = toeplitz(values, LON_DEV)
            conv = jnp.einsum('brjm,rnmc->nbjc', kernel.astype(jnp.float32), windows.astype(jnp.float32))
            conv = conv.astype(jnp.bfloat16)
            conv = jnp.transpose(conv, (1, 0, 2, 3)).reshape(count, NLON, C)
            result = rows_three[1].astype(jnp.float32) + jnp.einsum('bjc,bcd->jd', conv.astype(jnp.float32), weights_wide)
            return result.astype(jnp.bfloat16)
        return row_out
    top_rows = lax.map(make_row(WMAX), jnp.arange(POLAR).astype(jnp.int32))
    middle_rows = lax.map(make_row(NEAR), (jnp.arange(NLAT - 2 * POLAR) + POLAR).astype(jnp.int32))
    bottom_rows = lax.map(make_row(WMAX), (jnp.arange(POLAR) + NLAT - POLAR).astype(jnp.int32))
    return jnp.concatenate([top_rows, middle_rows, bottom_rows], 0)
```

```python
import functools

import jax
import jax.numpy as jnp
from jax import lax
from jax.experimental import pallas as pl
from jax.experimental.pallas import tpu as pltpu
from jax.sharding import PartitionSpec as P

MESH = pl.DeviceIdType.MESH
POLAR = 8
NEAR = 16
G = 8
LANES = 128
F32 = jnp.float32
BF16 = jnp.bfloat16


def mix_rows(conv, mix_v, ext, out_v, first):
    columns = out_v.shape[1]
    channels = out_v.shape[2]
    own = ext[pl.ds(first + 1, G), NEAR : NEAR + columns, :].astype(F32)
    mixed = jnp.dot(conv[...], mix_v[...], preferred_element_type=F32)
    result = own.reshape(G * columns, channels) + mixed
    out_v[pl.ds(first, G)] = result.reshape(G, columns, channels).astype(BF16)


def scale_of(width):
    return 1.0 / jnp.sqrt(3.0 * (2.0 * width.astype(F32) + 1.0))


def toeplitz_roll(row, columns, shift):
    return pltpu.roll(
        jnp.broadcast_to(row, (columns, LANES)), shift, 1, stride=1, stride_axis=0
    )


def kernel(
    feat, quad, cyc, widths, mix, out,
    ext, pol, quad_v, cyc_v, mix_v, w01, w2, c01, c2, conv, out_v,
    local, send, recv, lat_send, lat_recv, pol_send, pol_recv, out_sem,
):
    lat = lax.axis_index("lat")
    lon = lax.axis_index("lon")
    n_lat = lax.axis_size("lat")
    n_lon = lax.axis_size("lon")
    rows, columns, channels = feat.shape
    count = mix.shape[0]
    groups = rows // G
    span = columns + 2 * NEAR
    reach = quad.shape[2] // 2

    def lon_at(step):
        return lax.rem(lon + step + n_lon, n_lon)

    north = lat == 0
    south = lat == n_lat - 1
    polar = jnp.logical_or(north, south)
    even = lax.rem(lon, 2) == 0

    barrier = pltpu.get_barrier_semaphore()
    for step in (-1, 1):
        pl.semaphore_signal(barrier, 1, device_id=(lat, lon_at(step)), device_id_type=MESH)

    loads = [
        pltpu.make_async_copy(feat, ext.at[pl.ds(1, rows), pl.ds(NEAR, columns)], local.at[0]),
        pltpu.make_async_copy(quad, quad_v, local.at[1]),
        pltpu.make_async_copy(cyc, cyc_v, local.at[2]),
    ] + [
        pltpu.make_async_copy(
            mix.at[b], mix_v.at[pl.ds(b * channels, channels)], local.at[3 + b]
        )
        for b in range(count)
    ]

    @pl.when(polar)
    def _():
        for step in (-2, 2):
            pl.semaphore_signal(barrier, 1, device_id=(lat, lon_at(step)), device_id_type=MESH)

    @pl.when(jnp.logical_not(north))
    def _():
        pl.semaphore_signal(barrier, 1, device_id=(lat - 1, lon), device_id_type=MESH)

    @pl.when(jnp.logical_not(south))
    def _():
        pl.semaphore_signal(barrier, 1, device_id=(lat + 1, lon), device_id_type=MESH)

    for load in loads:
        load.start()
    pl.semaphore_wait(barrier, jnp.where(polar, 5, 4))

    def to_south():
        return pltpu.make_async_remote_copy(
            feat.at[pl.ds(rows - 1, 1)], ext.at[pl.ds(0, 1), pl.ds(NEAR, columns)],
            lat_send.at[0], lat_recv.at[0], (lat + 1, lon), MESH)

    def to_north():
        return pltpu.make_async_remote_copy(
            feat.at[pl.ds(0, 1)], ext.at[pl.ds(rows + 1, 1), pl.ds(NEAR, columns)],
            lat_send.at[1], lat_recv.at[1], (lat - 1, lon), MESH)

    @pl.when(jnp.logical_not(south))
    def _():
        to_south().start()

    @pl.when(jnp.logical_not(north))
    def _():
        to_north().start()

    need = POLAR + 1
    side = {True: (0, 1), False: (rows - need, 0)}

    def block(at_north, step):
        row = side[at_north][1]
        return pol.at[pl.ds(row, need), pl.ds((step + 2) * columns, columns)]

    def polar_copies(at_north, at_even):
        own = feat.at[pl.ds(side[at_north][0], need)]

        def copy(src, target, seen, slot):
            return pltpu.make_async_remote_copy(
                src, block(at_north, seen), pol_send.at[slot], pol_recv.at[seen + 2],
                (lat, lon_at(target)), MESH)

        far = 2 if at_even else -2
        near = 1 if at_even else -1
        first = [copy(own, far, -far, 0), copy(own, -near, near, 1), copy(own, near, -near, 2)]
        onward = copy(block(at_north, -near), near, -far, 3)
        return first, onward

    def pol_arrived(at_north, step):
        pltpu.make_async_copy(block(at_north, step), block(at_north, step), pol_recv.at[step + 2]).wait()

    cases = [(a, b) for a in (True, False) for b in (True, False)]

    def when_case(case):
        at_pole = north if case[0] else south
        parity = even if case[1] else jnp.logical_not(even)
        return pl.when(jnp.logical_and(at_pole, parity))

    for case in cases:
        @when_case(case)
        def _():
            for c in polar_copies(*case)[0]:
                c.start()

    def edge(way, row, length, slot, halo=False):
        start = (columns - NEAR) if way == 0 else 0
        if halo:
            src = ext.at[pl.ds(row, length), pl.ds(NEAR + start, NEAR)]
        else:
            src = feat.at[pl.ds(row - 1, length), pl.ds(start, NEAR)]
        land = 0 if way == 0 else NEAR + columns
        return pltpu.make_async_remote_copy(
            src, ext.at[pl.ds(row, length), pl.ds(land, NEAR)],
            send.at[way, slot], recv.at[way, slot],
            (lat, lon_at(1 if way == 0 else -1)), MESH)

    top, bottom = groups, groups + 1

    def both(action, row, length, slot, halo=False):
        for way in (0, 1):
            action(edge(way, row, length, slot, halo))

    def first_chunk(action):
        @pl.when(north)
        def _():
            both(action, G, 1, 0)

        @pl.when(jnp.logical_not(north))
        def _():
            both(action, 1, G, 0)

    def last_chunk(action):
        @pl.when(south)
        def _():
            both(action, rows - G + 1, 1, groups - 1)

        @pl.when(jnp.logical_not(south))
        def _():
            both(action, rows - G + 1, G, groups - 1)

    def chunk(action, g):
        both(action, g * G + 1, G, g)

    def top_row(action):
        @pl.when(jnp.logical_not(north))
        def _():
            both(action, 0, 1, top, True)

    def bottom_row(action):
        @pl.when(jnp.logical_not(south))
        def _():
            both(action, rows + 1, 1, bottom, True)

    def start(c):
        c.start()

    def wait_recv(c):
        c.wait_recv()

    def wait_send(c):
        c.wait_send()

    first_chunk(start)
    for g in range(1, 3):
        chunk(start, g)

    @pl.when(jnp.logical_not(north))
    def _():
        to_south().wait_recv()

    @pl.when(jnp.logical_not(south))
    def _():
        to_north().wait_recv()

    top_row(start)
    bottom_row(start)

    @pl.loop(3, groups - 1)
    def _(g):
        chunk(start, g)

    last_chunk(start)

    loads[1].wait()
    loads[2].wait()
    low = lax.broadcasted_iota(jnp.int32, (rows, LANES), 1) < span
    back = LANES - (reach - NEAR)

    def arrange(table):
        parts = [table[:, r, 0:LANES].astype(F32) for r in range(3)]
        first = pltpu.roll(parts[0], back, 1)
        second = pltpu.roll(parts[1], (back + span) % LANES, 1)
        return jnp.where(low, first, second), pltpu.roll(parts[2], back, 1)

    w01[...], w2[...] = arrange(quad_v)
    c01[...], c2[...] = arrange(cyc_v)

    lane = lax.broadcasted_iota(jnp.int32, (1, LANES), 1)
    near_offset = jnp.abs(lax.rem(lane, span) - NEAR)

    for load in loads[3:]:
        load.wait()
    loads[0].wait()

    def store_conv(value, k):
        for b in range(count):
            conv[k * columns : (k + 1) * columns, b * channels : (b + 1) * channels] = value[
                b * columns : (b + 1) * columns
            ]

    def banded(values, basis):
        zero = jnp.zeros_like(values)
        return jnp.concatenate(
            [jnp.where(basis == b, values, zero) for b in range(count)], axis=0
        )

    def emit(first, slot):
        copy = pltpu.make_async_copy(
            out_v.at[pl.ds(first, G)], out.at[pl.ds(first, G)], out_sem.at[slot])
        copy.start()

    def near_group(g):
        for k in range(G):
            i = g * G + k
            width = jnp.full((1, LANES), widths[i], jnp.int32)
            inside = near_offset <= width
            scale = scale_of(width)

            def spread(ref, weigh):
                row = ref[pl.ds(i, 1), :]
                if weigh:
                    row = jnp.where(inside, row, 0.0) * scale
                return toeplitz_roll(row, columns, 0)

            values = jnp.concatenate([spread(w01, True), spread(w2, True)], axis=1)
            basis = jnp.concatenate([spread(c01, False), spread(c2, False)], axis=1)
            values = values[:, : 3 * span].astype(BF16)
            basis = basis[:, : 3 * span].astype(BF16)
            window = ext[pl.ds(i, 3)].reshape(3 * span, channels)
            value = jnp.dot(banded(values, basis), window, preferred_element_type=F32)
            store_conv(value.astype(BF16), k)
        mix_rows(conv, mix_v, ext, out_v, g * G)
        emit(g * G, g)

    def polar_group(at_north):
        base = 0 if at_north else rows - POLAR
        own = pltpu.make_async_copy(
            feat.at[pl.ds(side[at_north][0], need)], block(at_north, 0), local.at[0])
        own.start()
        pol[0 if at_north else need] = jnp.zeros(pol.shape[1:], BF16)
        own.wait()
        line = lax.broadcasted_iota(jnp.int32, (columns, LANES), 0)
        across = lax.broadcasted_iota(jnp.int32, (columns, LANES), 1)
        kept = across >= line
        ahead = across == line

        for k in range(POLAR):
            width = jnp.full((1, LANES), widths[base + k], jnp.int32)
            inside = jnp.abs(lane - reach) <= width
            scale = scale_of(width)
            total = None
            for r in range(3):
                def spread(ref, weigh):
                    row = ref[base + k, r : r + 1, 0:LANES].astype(F32)
                    last = jnp.broadcast_to(
                        ref[base + k, r : r + 1, LANES : LANES + 1].astype(F32), (1, LANES))
                    if weigh:
                        row = jnp.where(inside, row, 0.0) * scale
                        last = jnp.where(width >= reach, last, 0.0) * scale
                    turned = toeplitz_roll(row, columns, 0)
                    return jnp.concatenate(
                        [
                            jnp.where(kept, turned, 0.0),
                            jnp.where(kept, jnp.where(ahead, last, 0.0), turned),
                        ],
                        axis=1,
                    )

                values = spread(quad_v, True)[:, : pol.shape[1]].astype(BF16)
                basis = spread(cyc_v, False)[:, : pol.shape[1]].astype(BF16)
                term = jnp.dot(banded(values, basis), pol[k + r], preferred_element_type=F32)
                total = term if total is None else total + term
            store_conv(total.astype(BF16), k)
        mix_rows(conv, mix_v, ext, out_v, base)
        emit(base, base // G)

    for case in cases:
        @when_case(case)
        def _():
            near = 1 if case[1] else -1
            pol_arrived(case[0], -near)
            polar_copies(*case)[1].start()
            for step in (near, 2, -2):
                pol_arrived(case[0], step)

    for at_north in (True, False):
        @pl.when(north if at_north else south)
        def _():
            polar_group(at_north)

    first_chunk(wait_recv)
    top_row(wait_recv)

    @pl.loop(0, groups)
    def _(g):
        @pl.when(g < groups - 2)
        def _():
            chunk(wait_recv, g + 1)

        @pl.when(g == groups - 2)
        def _():
            last_chunk(wait_recv)

        @pl.when(g == groups - 1)
        def _():
            bottom_row(wait_recv)

        skip = jnp.logical_or(
            jnp.logical_and(north, g == 0), jnp.logical_and(south, g == groups - 1))

        @pl.when(jnp.logical_not(skip))
        def _():
            near_group(g)

    first_chunk(wait_send)
    last_chunk(wait_send)
    top_row(wait_send)
    bottom_row(wait_send)

    @pl.loop(1, groups - 1)
    def _(g):
        chunk(wait_send, g)

    @pl.when(jnp.logical_not(south))
    def _():
        to_south().wait_send()

    @pl.when(jnp.logical_not(north))
    def _():
        to_north().wait_send()

    for case in cases:
        @when_case(case)
        def _():
            first, onward = polar_copies(*case)
            for c in first + [onward]:
                c.wait_send()

    @pl.loop(0, groups)
    def _(g):
        pltpu.make_async_copy(
            out_v.at[pl.ds(g * G, G)], out.at[pl.ds(g * G, G)], out_sem.at[g]).wait()


def body(features, quad_weights, cycle_index, widths, mix_weight):
    rows, columns, channels = features.shape
    count = mix_weight.shape[0]
    reach = quad_weights.shape[2] // 2
    groups = rows // G
    dma = pltpu.SemaphoreType.DMA
    anywhere = pl.BlockSpec(memory_space=pl.ANY)
    return pl.pallas_call(
        kernel,
        out_shape=jax.ShapeDtypeStruct(features.shape, BF16),
        in_specs=[anywhere] * 3 + [pl.BlockSpec(memory_space=pltpu.SMEM), anywhere],
        out_specs=anywhere,
        scratch_shapes=[
            pltpu.VMEM((rows + 2, columns + 2 * NEAR, channels), BF16),
            pltpu.VMEM((POLAR + 2, columns + 2 * reach, channels), BF16),
            pltpu.VMEM(quad_weights.shape, F32),
            pltpu.VMEM(cycle_index.shape, jnp.int32),
            pltpu.VMEM((count * channels, channels), BF16),
            pltpu.VMEM((rows, LANES), F32),
            pltpu.VMEM((rows, LANES), F32),
            pltpu.VMEM((rows, LANES), F32),
            pltpu.VMEM((rows, LANES), F32),
            pltpu.VMEM((G * columns, count * channels), BF16),
            pltpu.VMEM((rows, columns, channels), BF16),
            dma((3 + count,)),
            dma((2, groups + 2)),
            dma((2, groups + 2)),
            dma((2,)),
            dma((2,)),
            dma((4,)),
            dma((5,)),
            dma((groups,)),
        ],
        compiler_params=pltpu.CompilerParams(
            collective_id=0, has_side_effects=True, vmem_limit_bytes=40 * 2**20
        ),
    )(features, quad_weights, cycle_index, widths, mix_weight)


def solution(mesh):
    in_specs = (P("lat", "lon", None), P("lat", None, None), P("lat", None, None), P("lat"), P())
    out_specs = P("lat", "lon", None)
    return jax.shard_map(body, mesh=mesh, in_specs=in_specs, out_specs=out_specs, check_vma=False)
```

```python
import functools

import jax
import jax.numpy as jnp
from jax import lax
from jax.experimental import pallas as pl
from jax.experimental.pallas import tpu as pltpu
from jax.sharding import PartitionSpec as P

MESH = pl.DeviceIdType.MESH
POLAR = 8
NEAR = 16
G = 8
M = 16
LANES = 128
F32 = jnp.float32
BF16 = jnp.bfloat16


def mix_rows(conv, mix_v, ext, out_v, first):
    columns = out_v.shape[1]
    channels = out_v.shape[2]
    own = ext[pl.ds(first + 1, M), NEAR : NEAR + columns, :].astype(F32)
    mixed = jnp.dot(conv[pl.ds(first * columns, M * columns), :], mix_v[...], preferred_element_type=F32)
    result = own.reshape(M * columns, channels) + mixed
    out_v[pl.ds(first, M)] = result.reshape(M, columns, channels).astype(BF16)


def scale_of(width):
    return 1.0 / jnp.sqrt(3.0 * (2.0 * width.astype(F32) + 1.0))


def toeplitz_roll(row, columns, shift):
    return pltpu.roll(
        jnp.broadcast_to(row, (columns, LANES)), shift, 1, stride=1, stride_axis=0
    )


def kernel(
    feat, quad, cyc, widths_any, mix, out,
    ext, pol, quad_v, cyc_v, quad_t, cyc_t, widths, mix_v, w01, w2, c01, c2, conv, out_v,
    local, send, recv, lat_send, lat_recv, pol_send, pol_recv, out_sem,
):
    lat = lax.axis_index("lat")
    lon = lax.axis_index("lon")
    n_lat = lax.axis_size("lat")
    n_lon = lax.axis_size("lon")
    rows, columns, channels = feat.shape
    count = mix.shape[0]
    groups = rows // G
    span = columns + 2 * NEAR
    reach = quad.shape[1] // 2

    def lon_at(step):
        return lax.rem(lon + step + n_lon, n_lon)

    north = lat == 0
    south = lat == n_lat - 1
    polar = jnp.logical_or(north, south)
    even = lax.rem(lon, 2) == 0

    barrier = pltpu.get_barrier_semaphore()
    for step in (-1, 1):
        pl.semaphore_signal(barrier, 1, device_id=(lat, lon_at(step)), device_id_type=MESH)

    loads = [
        pltpu.make_async_copy(feat, ext.at[pl.ds(1, rows), pl.ds(NEAR, columns)], local.at[0]),
        pltpu.make_async_copy(quad, quad_v, local.at[1]),
        pltpu.make_async_copy(cyc, cyc_v, local.at[2]),
        pltpu.make_async_copy(widths_any, widths, local.at[3]),
    ] + [
        pltpu.make_async_copy(
            mix.at[b], mix_v.at[pl.ds(b * channels, channels)], local.at[4 + b]
        )
        for b in range(count)
    ]

    @pl.when(polar)
    def _():
        for step in (-2, 2):
            pl.semaphore_signal(barrier, 1, device_id=(lat, lon_at(step)), device_id_type=MESH)

    @pl.when(jnp.logical_not(north))
    def _():
        pl.semaphore_signal(barrier, 1, device_id=(lat - 1, lon), device_id_type=MESH)

    @pl.when(jnp.logical_not(south))
    def _():
        pl.semaphore_signal(barrier, 1, device_id=(lat + 1, lon), device_id_type=MESH)

    for load in loads:
        load.start()
    pl.semaphore_wait(barrier, jnp.where(polar, 5, 4))

    def to_south():
        return pltpu.make_async_remote_copy(
            feat.at[pl.ds(rows - 1, 1)], ext.at[pl.ds(0, 1), pl.ds(NEAR, columns)],
            lat_send.at[0], lat_recv.at[0], (lat + 1, lon), MESH)

    def to_north():
        return pltpu.make_async_remote_copy(
            feat.at[pl.ds(0, 1)], ext.at[pl.ds(rows + 1, 1), pl.ds(NEAR, columns)],
            lat_send.at[1], lat_recv.at[1], (lat - 1, lon), MESH)

    @pl.when(jnp.logical_not(south))
    def _():
        to_south().start()

    @pl.when(jnp.logical_not(north))
    def _():
        to_north().start()

    need = POLAR + 1
    side = {True: (0, 1), False: (rows - need, 0)}

    def block(at_north, step):
        row = side[at_north][1]
        return pol.at[pl.ds(row, need), pl.ds((step + 2) * columns, columns)]

    def polar_copies(at_north, at_even):
        own = feat.at[pl.ds(side[at_north][0], need)]

        def copy(src, target, seen, slot):
            return pltpu.make_async_remote_copy(
                src, block(at_north, seen), pol_send.at[slot], pol_recv.at[seen + 2],
                (lat, lon_at(target)), MESH)

        far = 2 if at_even else -2
        near = 1 if at_even else -1
        first = [copy(own, far, -far, 0), copy(own, -near, near, 1), copy(own, near, -near, 2)]
        onward = copy(block(at_north, -near), near, -far, 3)
        return first, onward

    def pol_arrived(at_north, step):
        pltpu.make_async_copy(block(at_north, step), block(at_north, step), pol_recv.at[step + 2]).wait()

    cases = [(a, b) for a in (True, False) for b in (True, False)]

    def when_case(case):
        at_pole = north if case[0] else south
        parity = even if case[1] else jnp.logical_not(even)
        return pl.when(jnp.logical_and(at_pole, parity))

    for case in cases:
        @when_case(case)
        def _():
            for c in polar_copies(*case)[0]:
                c.start()

    def edge(way, row, length, slot, halo=False):
        start = (columns - NEAR) if way == 0 else 0
        if halo:
            src = ext.at[pl.ds(row, length), pl.ds(NEAR + start, NEAR)]
        else:
            src = feat.at[pl.ds(row - 1, length), pl.ds(start, NEAR)]
        land = 0 if way == 0 else NEAR + columns
        return pltpu.make_async_remote_copy(
            src, ext.at[pl.ds(row, length), pl.ds(land, NEAR)],
            send.at[way, slot], recv.at[way, slot],
            (lat, lon_at(1 if way == 0 else -1)), MESH)

    top, bottom = groups, groups + 1

    def both(action, row, length, slot, halo=False):
        for way in (0, 1):
            action(edge(way, row, length, slot, halo))

    def first_chunk(action):
        @pl.when(north)
        def _():
            both(action, G, 1, 0)

        @pl.when(jnp.logical_not(north))
        def _():
            both(action, 1, G, 0)

    def last_chunk(action):
        @pl.when(south)
        def _():
            both(action, rows - G + 1, 1, groups - 1)

        @pl.when(jnp.logical_not(south))
        def _():
            both(action, rows - G + 1, G, groups - 1)

    def chunk(action, g):
        both(action, g * G + 1, G, g)

    def top_row(action):
        @pl.when(jnp.logical_not(north))
        def _():
            both(action, 0, 1, top, True)

    def bottom_row(action):
        @pl.when(jnp.logical_not(south))
        def _():
            both(action, rows + 1, 1, bottom, True)

    def start(c):
        c.start()

    def wait_recv(c):
        c.wait_recv()

    def wait_send(c):
        c.wait_send()

    first_chunk(start)
    for g in range(1, 3):
        chunk(start, g)

    @pl.when(jnp.logical_not(north))
    def _():
        to_south().wait_recv()

    @pl.when(jnp.logical_not(south))
    def _():
        to_north().wait_recv()

    top_row(start)
    bottom_row(start)

    @pl.loop(3, groups - 1)
    def _(g):
        chunk(start, g)

    last_chunk(start)

    loads[1].wait()
    loads[2].wait()
    loads[3].wait()
    low = lax.broadcasted_iota(jnp.int32, (rows, LANES), 1) < span
    back = LANES - (reach - NEAR)

    def arrange(table, turned):
        parts = [jnp.swapaxes(table[r, 0:LANES, :].astype(F32), 0, 1) for r in range(3)]
        for r in range(3):
            turned[r] = parts[r]
        first = pltpu.roll(parts[0], back, 1)
        second = pltpu.roll(parts[1], (back + span) % LANES, 1)
        return jnp.where(low, first, second), pltpu.roll(parts[2], back, 1)

    w01[...], w2[...] = arrange(quad_v, quad_t)
    c01[...], c2[...] = arrange(cyc_v, cyc_t)

    lane = lax.broadcasted_iota(jnp.int32, (1, LANES), 1)
    near_offset = jnp.abs(lax.rem(lane, span) - NEAR)

    for load in loads[4:]:
        load.wait()
    loads[0].wait()

    def store_conv(value, i):
        for b in range(count):
            conv[pl.ds(i * columns, columns), b * channels : (b + 1) * channels] = value[
                b * columns : (b + 1) * columns
            ]

    def banded(values, basis):
        zero = jnp.zeros_like(values)
        return jnp.concatenate(
            [jnp.where(basis == b, values, zero) for b in range(count)], axis=0
        )

    def emit(first, slot):
        copy = pltpu.make_async_copy(
            out_v.at[pl.ds(first, M)], out.at[pl.ds(first, M)], out_sem.at[slot])
        copy.start()

    def near_group(g):
        for k in range(G):
            i = g * G + k
            width = jnp.full((1, LANES), widths[i], jnp.int32)
            inside = near_offset <= width
            scale = scale_of(width)

            def spread(ref, weigh):
                row = ref[pl.ds(i, 1), :]
                if weigh:
                    row = jnp.where(inside, row, 0.0) * scale
                return toeplitz_roll(row, columns, 0)

            values = jnp.concatenate([spread(w01, True), spread(w2, True)], axis=1)
            basis = jnp.concatenate([spread(c01, False), spread(c2, False)], axis=1)
            values = values[:, : 3 * span].astype(BF16)
            basis = basis[:, : 3 * span].astype(BF16)
            window = ext[pl.ds(i, 3)].reshape(3 * span, channels)
            value = jnp.dot(banded(values, basis), window, preferred_element_type=F32)
            store_conv(value.astype(BF16), i)

    def polar_group(at_north):
        base = 0 if at_north else rows - POLAR
        own = pltpu.make_async_copy(
            feat.at[pl.ds(side[at_north][0], need)], block(at_north, 0), local.at[0])
        own.start()
        pol[0 if at_north else need] = jnp.zeros(pol.shape[1:], BF16)
        own.wait()
        line = lax.broadcasted_iota(jnp.int32, (columns, LANES), 0)
        across = lax.broadcasted_iota(jnp.int32, (columns, LANES), 1)
        kept = across >= line
        ahead = across == line

        for k in range(POLAR):
            width = jnp.full((1, LANES), widths[base + k], jnp.int32)
            inside = jnp.abs(lane - reach) <= width
            scale = scale_of(width)
            total = None
            for r in range(3):
                def spread(ref, table, weigh):
                    i = base + k
                    row = ref[r, i : i + 1, :]
                    last = jnp.broadcast_to(
                        table[r, LANES : LANES + 1, i : i + 1].astype(F32), (1, LANES))
                    if weigh:
                        row = jnp.where(inside, row, 0.0) * scale
                        last = jnp.where(width >= reach, last, 0.0) * scale
                    turned = toeplitz_roll(row, columns, 0)
                    return jnp.concatenate(
                        [
                            jnp.where(kept, turned, 0.0),
                            jnp.where(kept, jnp.where(ahead, last, 0.0), turned),
                        ],
                        axis=1,
                    )

                values = spread(quad_t, quad_v, True)[:, : pol.shape[1]].astype(BF16)
                basis = spread(cyc_t, cyc_v, False)[:, : pol.shape[1]].astype(BF16)
                term = jnp.dot(banded(values, basis), pol[k + r], preferred_element_type=F32)
                total = term if total is None else total + term
            store_conv(total.astype(BF16), base + k)

    for case in cases:
        @when_case(case)
        def _():
            near = 1 if case[1] else -1
            pol_arrived(case[0], -near)
            polar_copies(*case)[1].start()
            for step in (near, 2, -2):
                pol_arrived(case[0], step)

    for at_north in (True, False):
        @pl.when(north if at_north else south)
        def _():
            polar_group(at_north)

    first_chunk(wait_recv)
    top_row(wait_recv)

    @pl.loop(0, groups)
    def _(g):
        @pl.when(g < groups - 2)
        def _():
            chunk(wait_recv, g + 1)

        @pl.when(g == groups - 2)
        def _():
            last_chunk(wait_recv)

        @pl.when(g == groups - 1)
        def _():
            bottom_row(wait_recv)

        skip = jnp.logical_or(
            jnp.logical_and(north, g == 0), jnp.logical_and(south, g == groups - 1))

        @pl.when(jnp.logical_not(skip))
        def _():
            near_group(g)

        @pl.when(lax.rem(g, M // G) == M // G - 1)
        def _():
            first = (g - (M // G - 1)) * G
            mix_rows(conv, mix_v, ext, out_v, first)
            emit(first, g // (M // G))

    first_chunk(wait_send)
    last_chunk(wait_send)
    top_row(wait_send)
    bottom_row(wait_send)

    @pl.loop(1, groups - 1)
    def _(g):
        chunk(wait_send, g)

    @pl.when(jnp.logical_not(south))
    def _():
        to_south().wait_send()

    @pl.when(jnp.logical_not(north))
    def _():
        to_north().wait_send()

    for case in cases:
        @when_case(case)
        def _():
            first, onward = polar_copies(*case)
            for c in first + [onward]:
                c.wait_send()

    @pl.loop(0, rows // M)
    def _(g):
        pltpu.make_async_copy(
            out_v.at[pl.ds(g * M, M)], out.at[pl.ds(g * M, M)], out_sem.at[g]).wait()


def body(features, quad_weights, cycle_index, widths, mix_weight):
    rows, columns, channels = features.shape
    count = mix_weight.shape[0]
    reach = quad_weights.shape[2] // 2
    quad = jnp.transpose(quad_weights, (1, 2, 0))
    cyc = jnp.transpose(cycle_index, (1, 2, 0))
    groups = rows // G
    dma = pltpu.SemaphoreType.DMA
    anywhere = pl.BlockSpec(memory_space=pl.ANY)
    return pl.pallas_call(
        kernel,
        out_shape=jax.ShapeDtypeStruct(features.shape, BF16),
        in_specs=[anywhere] * 5,
        out_specs=anywhere,
        scratch_shapes=[
            pltpu.VMEM((rows + 2, columns + 2 * NEAR, channels), BF16),
            pltpu.VMEM((POLAR + 2, columns + 2 * reach, channels), BF16),
            pltpu.VMEM(quad.shape, F32),
            pltpu.VMEM(cyc.shape, jnp.int32),
            pltpu.VMEM((3, rows, LANES), F32),
            pltpu.VMEM((3, rows, LANES), F32),
            pltpu.SMEM((rows,), jnp.int32),
            pltpu.VMEM((count * channels, channels), BF16),
            pltpu.VMEM((rows, LANES), F32),
            pltpu.VMEM((rows, LANES), F32),
            pltpu.VMEM((rows, LANES), F32),
            pltpu.VMEM((rows, LANES), F32),
            pltpu.VMEM((rows * columns, count * channels), BF16),
            pltpu.VMEM((rows, columns, channels), BF16),
            dma((4 + count,)),
            dma((2, groups + 2)),
            dma((2, groups + 2)),
            dma((2,)),
            dma((2,)),
            dma((4,)),
            dma((5,)),
            dma((rows // M,)),
        ],
        compiler_params=pltpu.CompilerParams(
            collective_id=0, has_side_effects=True, vmem_limit_bytes=60 * 2**20
        ),
    )(features, quad, cyc, widths, mix_weight)


def solution(mesh):
    in_specs = (P("lat", "lon", None), P("lat", None, None), P("lat", None, None), P("lat"), P())
    out_specs = P("lat", "lon", None)
    return jax.shard_map(body, mesh=mesh, in_specs=in_specs, out_specs=out_specs, check_vma=False)
```

```python
import functools

import jax
import jax.numpy as jnp
from jax import lax
from jax.experimental import pallas as pl
from jax.experimental.pallas import tpu as pltpu
from jax.sharding import PartitionSpec as P

MESH = pl.DeviceIdType.MESH
POLAR = 8
NEAR = 16
G = 8
M = 16
LANES = 128
F32 = jnp.float32
BF16 = jnp.bfloat16


def mix_rows(conv, mix_v, ext, out_v, first):
    columns = out_v.shape[1]
    channels = out_v.shape[2]
    own = ext[pl.ds(first + 1, M), NEAR : NEAR + columns, :].astype(F32)
    mixed = jnp.dot(conv[pl.ds(first * columns, M * columns), :], mix_v[...], preferred_element_type=F32)
    result = own.reshape(M * columns, channels) + mixed
    out_v[pl.ds(first, M)] = result.reshape(M, columns, channels).astype(BF16)


def scale_of(width):
    return 1.0 / jnp.sqrt(3.0 * (2.0 * width.astype(F32) + 1.0))


def toeplitz_roll(row, columns, shift):
    return pltpu.roll(
        jnp.broadcast_to(row, (columns, LANES)), shift, 1, stride=1, stride_axis=0
    )


def kernel(
    feat, quad, cyc, widths_any, mix, out,
    ext, pol, quad_v, cyc_v, quad_t, cyc_t, widths, mix_v, w01, w2, c01, c2, conv, out_v,
    local, send, recv, lat_send, lat_recv, pol_send, pol_recv, out_sem,
):
    lat = lax.axis_index("lat")
    lon = lax.axis_index("lon")
    n_lat = lax.axis_size("lat")
    n_lon = lax.axis_size("lon")
    rows, columns, channels = feat.shape
    count = mix.shape[0]
    groups = rows // G
    span = columns + 2 * NEAR
    reach = quad.shape[1] // 2

    def lon_at(step):
        return lax.rem(lon + step + n_lon, n_lon)

    north = lat == 0
    south = lat == n_lat - 1
    polar = jnp.logical_or(north, south)
    even = lax.rem(lon, 2) == 0

    barrier = pltpu.get_barrier_semaphore()
    for step in (-1, 1):
        pl.semaphore_signal(barrier, 1, device_id=(lat, lon_at(step)), device_id_type=MESH)

    loads = [
        pltpu.make_async_copy(feat, ext.at[pl.ds(1, rows), pl.ds(NEAR, columns)], local.at[0]),
        pltpu.make_async_copy(quad, quad_v, local.at[1]),
        pltpu.make_async_copy(cyc, cyc_v, local.at[2]),
        pltpu.make_async_copy(widths_any, widths, local.at[3]),
    ] + [
        pltpu.make_async_copy(
            mix.at[b], mix_v.at[pl.ds(b * channels, channels)], local.at[4 + b]
        )
        for b in range(count)
    ]

    @pl.when(polar)
    def _():
        for step in (-2, 2):
            pl.semaphore_signal(barrier, 1, device_id=(lat, lon_at(step)), device_id_type=MESH)

    @pl.when(jnp.logical_not(north))
    def _():
        pl.semaphore_signal(barrier, 1, device_id=(lat - 1, lon), device_id_type=MESH)

    @pl.when(jnp.logical_not(south))
    def _():
        pl.semaphore_signal(barrier, 1, device_id=(lat + 1, lon), device_id_type=MESH)

    for load in loads:
        load.start()
    pl.semaphore_wait(barrier, jnp.where(polar, 5, 4))

    def to_south():
        return pltpu.make_async_remote_copy(
            feat.at[pl.ds(rows - 1, 1)], ext.at[pl.ds(0, 1), pl.ds(NEAR, columns)],
            lat_send.at[0], lat_recv.at[0], (lat + 1, lon), MESH)

    def to_north():
        return pltpu.make_async_remote_copy(
            feat.at[pl.ds(0, 1)], ext.at[pl.ds(rows + 1, 1), pl.ds(NEAR, columns)],
            lat_send.at[1], lat_recv.at[1], (lat - 1, lon), MESH)

    @pl.when(jnp.logical_not(south))
    def _():
        to_south().start()

    @pl.when(jnp.logical_not(north))
    def _():
        to_north().start()

    need = POLAR + 1
    side = {True: (0, 1), False: (rows - need, 0)}

    def block(at_north, step):
        row = side[at_north][1]
        return pol.at[pl.ds(row, need), pl.ds((step + 2) * columns, columns)]

    def polar_copies(at_north, at_even):
        own = feat.at[pl.ds(side[at_north][0], need)]

        def copy(src, target, seen, slot):
            return pltpu.make_async_remote_copy(
                src, block(at_north, seen), pol_send.at[slot], pol_recv.at[seen + 2],
                (lat, lon_at(target)), MESH)

        far = 2 if at_even else -2
        near = 1 if at_even else -1
        first = [copy(own, far, -far, 0), copy(own, -near, near, 1), copy(own, near, -near, 2)]
        onward = copy(block(at_north, -near), near, -far, 3)
        return first, onward

    def pol_arrived(at_north, step):
        pltpu.make_async_copy(block(at_north, step), block(at_north, step), pol_recv.at[step + 2]).wait()

    cases = [(a, b) for a in (True, False) for b in (True, False)]

    def when_case(case):
        at_pole = north if case[0] else south
        parity = even if case[1] else jnp.logical_not(even)
        return pl.when(jnp.logical_and(at_pole, parity))

    for case in cases:
        @when_case(case)
        def _():
            for c in polar_copies(*case)[0]:
                c.start()

    def edge(way, row, length, slot, halo=False):
        start = (columns - NEAR) if way == 0 else 0
        if halo:
            src = ext.at[pl.ds(row, length), pl.ds(NEAR + start, NEAR)]
        else:
            src = feat.at[pl.ds(row - 1, length), pl.ds(start, NEAR)]
        land = 0 if way == 0 else NEAR + columns
        return pltpu.make_async_remote_copy(
            src, ext.at[pl.ds(row, length), pl.ds(land, NEAR)],
            send.at[way, slot], recv.at[way, slot],
            (lat, lon_at(1 if way == 0 else -1)), MESH)

    top, bottom = groups, groups + 1

    def both(action, row, length, slot, halo=False):
        for way in (0, 1):
            action(edge(way, row, length, slot, halo))

    def first_chunk(action):
        @pl.when(north)
        def _():
            both(action, G, 1, 0)

        @pl.when(jnp.logical_not(north))
        def _():
            both(action, 1, G, 0)

    def last_chunk(action):
        @pl.when(south)
        def _():
            both(action, rows - G + 1, 1, groups - 1)

        @pl.when(jnp.logical_not(south))
        def _():
            both(action, rows - G + 1, G, groups - 1)

    def chunk(action, g):
        both(action, g * G + 1, G, g)

    def top_row(action):
        @pl.when(jnp.logical_not(north))
        def _():
            both(action, 0, 1, top, True)

    def bottom_row(action):
        @pl.when(jnp.logical_not(south))
        def _():
            both(action, rows + 1, 1, bottom, True)

    def start(c):
        c.start()

    def wait_recv(c):
        c.wait_recv()

    def wait_send(c):
        c.wait_send()

    first_chunk(start)
    for g in range(1, 3):
        chunk(start, g)

    @pl.when(jnp.logical_not(north))
    def _():
        to_south().wait_recv()

    @pl.when(jnp.logical_not(south))
    def _():
        to_north().wait_recv()

    top_row(start)
    bottom_row(start)

    @pl.loop(3, groups - 1)
    def _(g):
        chunk(start, g)

    last_chunk(start)

    loads[1].wait()
    loads[2].wait()
    loads[3].wait()
    low = lax.broadcasted_iota(jnp.int32, (rows, LANES), 1) < span
    back = LANES - (reach - NEAR)

    def arrange(table, turned):
        parts = [jnp.swapaxes(table[r, 0:LANES, :].astype(F32), 0, 1) for r in range(3)]
        for r in range(3):
            turned[r] = parts[r]
        first = pltpu.roll(parts[0], back, 1)
        second = pltpu.roll(parts[1], (back + span) % LANES, 1)
        return jnp.where(low, first, second), pltpu.roll(parts[2], back, 1)

    w01[...], w2[...] = arrange(quad_v, quad_t)
    c01[...], c2[...] = arrange(cyc_v, cyc_t)

    lane = lax.broadcasted_iota(jnp.int32, (1, LANES), 1)
    near_offset = jnp.abs(lax.rem(lane, span) - NEAR)

    for load in loads[4:]:
        load.wait()
    loads[0].wait()

    def store_conv(value, i):
        for b in range(count):
            conv[pl.ds(i * columns, columns), b * channels : (b + 1) * channels] = value[
                b * columns : (b + 1) * columns
            ]

    def banded(values, basis):
        zero = jnp.zeros_like(values)
        return jnp.concatenate(
            [jnp.where(basis == b, values, zero) for b in range(count)], axis=0
        )

    def emit(first, slot):
        copy = pltpu.make_async_copy(
            out_v.at[pl.ds(first, M)], out.at[pl.ds(first, M)], out_sem.at[slot])
        copy.start()

    def near_group(g):
        for k in range(G):
            i = g * G + k
            width = jnp.full((1, LANES), widths[i], jnp.int32)
            inside = near_offset <= width
            scale = scale_of(width)

            def spread(ref, weigh):
                row = ref[pl.ds(i, 1), :]
                if weigh:
                    row = jnp.where(inside, row, 0.0) * scale
                return toeplitz_roll(row, columns, 0)

            values = jnp.concatenate([spread(w01, True), spread(w2, True)], axis=1)
            basis = jnp.concatenate([spread(c01, False), spread(c2, False)], axis=1)
            values = values[:, : 3 * span].astype(BF16)
            basis = basis[:, : 3 * span].astype(BF16)
            window = ext[pl.ds(i, 3)].reshape(3 * span, channels)
            value = jnp.dot(banded(values, basis), window, preferred_element_type=F32)
            store_conv(value.astype(BF16), i)

    def polar_group(at_north):
        base = 0 if at_north else rows - POLAR
        own = pltpu.make_async_copy(
            feat.at[pl.ds(side[at_north][0], need)], block(at_north, 0), local.at[0])
        own.start()
        pol[0 if at_north else need] = jnp.zeros(pol.shape[1:], BF16)
        own.wait()
        line = lax.broadcasted_iota(jnp.int32, (columns, LANES), 0)
        across = lax.broadcasted_iota(jnp.int32, (columns, LANES), 1)
        kept = across >= line
        ahead = across == line

        for k in range(POLAR):
            width = jnp.full((1, LANES), widths[base + k], jnp.int32)
            inside = jnp.abs(lane - reach) <= width
            scale = scale_of(width)
            total = None
            for r in range(3):
                def spread(ref, table, weigh):
                    i = base + k
                    row = ref[r, i : i + 1, :]
                    last = jnp.broadcast_to(
                        table[r, LANES : LANES + 1, i : i + 1].astype(F32), (1, LANES))
                    if weigh:
                        row = jnp.where(inside, row, 0.0) * scale
                        last = jnp.where(width >= reach, last, 0.0) * scale
                    turned = toeplitz_roll(row, columns, 0)
                    return jnp.concatenate(
                        [
                            jnp.where(kept, turned, 0.0),
                            jnp.where(kept, jnp.where(ahead, last, 0.0), turned),
                        ],
                        axis=1,
                    )

                values = spread(quad_t, quad_v, True)[:, : pol.shape[1]].astype(BF16)
                basis = spread(cyc_t, cyc_v, False)[:, : pol.shape[1]].astype(BF16)
                term = jnp.dot(banded(values, basis), pol[k + r], preferred_element_type=F32)
                total = term if total is None else total + term
            store_conv(total.astype(BF16), base + k)

    for case in cases:
        @when_case(case)
        def _():
            near = 1 if case[1] else -1
            pol_arrived(case[0], -near)
            polar_copies(*case)[1].start()
            for step in (near, 2, -2):
                pol_arrived(case[0], step)

    for at_north in (True, False):
        @pl.when(north if at_north else south)
        def _():
            polar_group(at_north)

    first_chunk(wait_recv)
    top_row(wait_recv)

    @pl.loop(0, groups)
    def _(g):
        @pl.when(g < groups - 2)
        def _():
            chunk(wait_recv, g + 1)

        @pl.when(g == groups - 2)
        def _():
            last_chunk(wait_recv)

        @pl.when(g == groups - 1)
        def _():
            bottom_row(wait_recv)

        skip = jnp.logical_or(
            jnp.logical_and(north, g == 0), jnp.logical_and(south, g == groups - 1))

        @pl.when(jnp.logical_not(skip))
        def _():
            near_group(g)

        @pl.when(lax.rem(g, M // G) == M // G - 1)
        def _():
            first = (g - (M // G - 1)) * G
            mix_rows(conv, mix_v, ext, out_v, first)
            emit(first, g // (M // G))

    first_chunk(wait_send)
    last_chunk(wait_send)
    top_row(wait_send)
    bottom_row(wait_send)

    @pl.loop(1, groups - 1)
    def _(g):
        chunk(wait_send, g)

    @pl.when(jnp.logical_not(south))
    def _():
        to_south().wait_send()

    @pl.when(jnp.logical_not(north))
    def _():
        to_north().wait_send()

    for case in cases:
        @when_case(case)
        def _():
            first, onward = polar_copies(*case)
            for c in first + [onward]:
                c.wait_send()

    @pl.loop(0, rows // M)
    def _(g):
        pltpu.make_async_copy(
            out_v.at[pl.ds(g * M, M)], out.at[pl.ds(g * M, M)], out_sem.at[g]).wait()


def move(source, out, held, into, back):
    pieces = range(source.shape[0] // G)
    ins = [
        pltpu.make_async_copy(source.at[pl.ds(g * G, G)], held.at[pl.ds(g * G, G)], into.at[g])
        for g in pieces
    ]
    outs = [
        pltpu.make_async_copy(held.at[pl.ds(g * G, G)], out.at[pl.ds(g * G, G)], back.at[g])
        for g in pieces
    ]
    for copy in ins:
        copy.start()
    for first, second in zip(ins, outs):
        first.wait()
        second.start()
    for copy in outs:
        copy.wait()


def body(features, quad_weights, cycle_index, widths, mix_weight):
    rows, columns, channels = features.shape
    count = mix_weight.shape[0]
    reach = quad_weights.shape[2] // 2
    quad = jnp.transpose(quad_weights, (1, 2, 0))
    cyc = jnp.transpose(cycle_index, (1, 2, 0))
    groups = rows // G
    dma = pltpu.SemaphoreType.DMA
    anywhere = pl.BlockSpec(memory_space=pl.ANY)
    mixed = pl.pallas_call(
        kernel,
        out_shape=jax.ShapeDtypeStruct(features.shape, BF16),
        in_specs=[anywhere] * 5,
        out_specs=anywhere,
        scratch_shapes=[
            pltpu.VMEM((rows + 2, columns + 2 * NEAR, channels), BF16),
            pltpu.VMEM((POLAR + 2, columns + 2 * reach, channels), BF16),
            pltpu.VMEM(quad.shape, F32),
            pltpu.VMEM(cyc.shape, jnp.int32),
            pltpu.VMEM((3, rows, LANES), F32),
            pltpu.VMEM((3, rows, LANES), F32),
            pltpu.SMEM((rows,), jnp.int32),
            pltpu.VMEM((count * channels, channels), BF16),
            pltpu.VMEM((rows, LANES), F32),
            pltpu.VMEM((rows, LANES), F32),
            pltpu.VMEM((rows, LANES), F32),
            pltpu.VMEM((rows, LANES), F32),
            pltpu.VMEM((rows * columns, count * channels), BF16),
            pltpu.VMEM((rows, columns, channels), BF16),
            dma((4 + count,)),
            dma((2, groups + 2)),
            dma((2, groups + 2)),
            dma((2,)),
            dma((2,)),
            dma((4,)),
            dma((5,)),
            dma((rows // M,)),
        ],
        compiler_params=pltpu.CompilerParams(
            collective_id=0, has_side_effects=True, vmem_limit_bytes=60 * 2**20
        ),
    )(features, quad, cyc, widths, mix_weight)
    return pl.pallas_call(
        move,
        out_shape=jax.ShapeDtypeStruct(features.shape, BF16),
        in_specs=[anywhere],
        out_specs=anywhere,
        scratch_shapes=[pltpu.VMEM(features.shape, BF16), dma((groups,)), dma((groups,))],
        compiler_params=pltpu.CompilerParams(vmem_limit_bytes=60 * 2**20),
    )(mixed)


def solution(mesh):
    in_specs = (P("lat", "lon", None), P("lat", None, None), P("lat", None, None), P("lat"), P())
    out_specs = P("lat", "lon", None)
    return jax.shard_map(body, mesh=mesh, in_specs=in_specs, out_specs=out_specs, check_vma=False)
```
